32 devices in a mesh: fsdp: 32 (over z, y, x, core).
Axes of the slice: x: 2, y: 2, z: 4, core: 2. Of those that a mesh axis runs over, the one named last changes fastest.
Arguments:
- tokens: bfloat16 [12608, 768], P('fsdp'), may hold values from -6 to 6
- ln1_gain: bfloat16 [768], P('fsdp'), may hold values from 0.5 to 1.5
- ln1_shift: bfloat16 [768], P('fsdp'), may hold values from -3 to 3
- qkv_weight: bfloat16 [768, 2304], P('fsdp'), may hold values from -0.21875 to 0.21875
- qv_bias: bfloat16 [2, 768], P(None, 'fsdp'), may hold values from -3 to 3
- proj_weight: bfloat16 [768, 768], P('fsdp'), may hold values from -1 to 1
- proj_bias: bfloat16 [768], P('fsdp'), may hold values from -3 to 3
- ln2_gain: bfloat16 [768], P('fsdp'), may hold values from 0.5 to 1.5
- ln2_shift: bfloat16 [768], P('fsdp'), may hold values from -3 to 3
- router_weight: bfloat16 [768, 4], P('fsdp'), may hold values from -0.15625 to 0.15625
- expert_in: bfloat16 [3072, 4, 768], P('fsdp'), may hold values from -0.21875 to 0.21875
- expert_in_bias: bfloat16 [3072, 4], P('fsdp'), may hold values from -3 to 3
- expert_out: bfloat16 [3072, 4, 768], P('fsdp'), may hold values from -0.3125 to 0.3125
- expert_out_bias: bfloat16 [4, 768], P(None, 'fsdp'), may hold values from -3 to 3
- routes: int32 [12608, 2], P('fsdp'), may hold values from 0 to 3, all different within a row; in each aligned block of 394 rows (0 to 393, 394 to 787, ...) at most 246 rows name the same one
- out_grad: bfloat16 [12608, 768], P('fsdp'), may hold values from -6 to 6
Outputs:
- block_out: bfloat16 [12608, 768], P('fsdp')
- tokens_grad: float32 [12608, 768], P('fsdp')
- ln1_gain_grad: float32 [768], P('fsdp')
- ln1_shift_grad: float32 [768], P('fsdp')
- qkv_weight_grad: float32 [768, 2304], P('fsdp')
- qv_bias_grad: float32 [2, 768], P(None, 'fsdp')
- proj_weight_grad: float32 [768, 768], P('fsdp')
- proj_bias_grad: float32 [768], P('fsdp')
- ln2_gain_grad: float32 [768], P('fsdp')
- ln2_shift_grad: float32 [768], P('fsdp')
- router_weight_grad: float32 [768, 4], P('fsdp')
- expert_in_grad: float32 [3072, 4, 768], P('fsdp')
- expert_in_bias_grad: float32 [3072, 4], P('fsdp')
- expert_out_grad: float32 [3072, 4, 768], P('fsdp')
- expert_out_bias_grad: float32 [4, 768], P(None, 'fsdp')
The draws below stay inside these ranges and needn't reach their ends.
Inputs may be any that keep to these rules, and one draw needn't show every extreme that they name: `routes`: each row names 2 different experts. Within the rows of one device no expert is named more than 246 times, and in some blocks one expert is named exactly 246 times.
All inputs are finite; a program needn't handle non-finite values.
Results may differ from the reference program's by a relative error of at most 0.015.
Values may be sent and summed in bfloat16 or wider, within the bound.
A program may use at most 320 MiB of HBM per device.

```python
import math
import jax
import jax.numpy as jnp
import numpy as np
from jax import lax

D = 768
HEADS = 12
HD = 64
FF = 3072
EXPERTS = 4
TOP = 2
LEN = 197
SEQ_DEV = 2
TOK_DEV = 394
CAP = 246
TOKENS = 12608
N_FSDP = 32


def strengthened(values, stream_key, source, target, parts, factor):
    owner, partner = [(jnp.arange(values.shape[position]) // (values.shape[position] // parts)).reshape([-1 if axis == position else 1 for axis in range(values.ndim)]) for position in (source, target)]
    chosen = jax.random.permutation(stream_key, parts)[partner]
    strong = (owner == chosen) | (owner == (partner + parts // 2) % parts)
    return jnp.where(strong, factor * values, values)


def levels(own_key, dims, split, smallest, top_value):
    loudness, own = 1.0, jax.random.fold_in(own_key, 6)
    for position, blocks in split:
        draws = jnp.exp(jax.random.uniform(jax.random.fold_in(own, position), (blocks,), jnp.float32, smallest / len(split), top_value / len(split)))
        loudness = loudness * jnp.repeat(draws, dims[position] // blocks).reshape([-1 if axis == position else 1 for axis in range(len(dims))])
    return loudness


def deal_out(rng, own, number, rows, count, top, most, slope):
    sequence = jax.random.permutation(rng, count)
    heavy_load, common = load_shares(count, rows * top, most, slope, True), load_shares(count, rows * top, most, slope, False)
    places = jnp.arange(count)

    def named(lengths, offset_by):
        used = int((lengths > 0).sum())
        fixed = max(1, used // 4)
        shifted = fixed + (places - fixed + offset_by * (used - fixed)) % max(1, count - fixed)
        return jnp.zeros((count,), jnp.int32).at[sequence[jnp.where(places < fixed, places, shifted)]].set(jnp.asarray(lengths, jnp.int32))

    lengths = jnp.where(number % 4 == 0, named(heavy_load, number // 4), named(common, number - number // 4 - 1))
    mixed = jax.random.permutation(jax.random.fold_in(own, 3), count)
    giver, sink = mixed[0:count // 2 * 2:2], mixed[1:count // 2 * 2:2]
    slack = jnp.minimum(lengths[giver] - 1, most - lengths[sink]) // 2
    slack = jnp.where((giver == sequence[0]) | (sink == sequence[0]) | (lengths[sink] == 0), 0, jnp.maximum(slack, 0))
    shifted = jax.random.randint(jax.random.fold_in(own, 4), (count // 2,), 0, 1 << 20) % (slack + 1)
    lengths = lengths.at[giver].add(-shifted).at[sink].add(shifted)
    members = jnp.searchsorted(jnp.cumsum(lengths), jnp.arange(rows * top), side="right").astype(jnp.int32)
    grid = members.reshape(top, rows).T
    grid = grid[jax.random.permutation(jax.random.fold_in(own, 1), rows)]
    offset_by = jax.random.randint(jax.random.fold_in(own, 2), (rows, 1), 0, top)
    return jnp.take_along_axis(grid, (jnp.arange(top)[None, :] + offset_by) % top, axis=1)


def load_shares(number_of, total, limit, lean, full):
    portions = [(1 << 20) // math.isqrt(rank ** lean) + 1 for rank in range(1, number_of + 1)]
    largest = limit if full else min(limit, max(-(-total // number_of), total * portions[0] // sum(portions)))
    least = 1 if total - largest >= number_of - 1 else 0
    counts, surplus = [largest] + [least] * (number_of - 1), total - largest - least * (number_of - 1)
    while surplus > 0:
        candidates = [i for i in range(1, number_of) if counts[i] < largest] or [i for i in range(1, number_of) if counts[i] < limit]
        whole, budget = sum([portions[i] for i in candidates]), surplus
        for i in candidates:
            addition = min(limit - counts[i], max(1, budget * portions[i] // whole), surplus)
            counts[i] = counts[i] + addition
            surplus = surplus - addition
    return np.array(counts)


def bell_draw(key, dims, scale, limit, shards=(), kind=jnp.bfloat16):
    array = scale * jax.random.normal(key, dims, jnp.float32)
    if shards:
        array = array * levels(key, dims, shards, -0.22, 0.18)
    return jnp.clip(array, -limit, limit).astype(kind)


def heavy_noise(rng, extent, scale, bound, pieces, heavy, kind=jnp.bfloat16):
    values = scale * jax.random.normal(rng, extent, jnp.float32)
    if pieces:
        values = values * levels(rng, extent, pieces, -0.22, 0.18)
    return jnp.clip(strengthened(values, jax.random.fold_in(rng, 3), *heavy), -bound, bound).astype(kind)


def setup_inputs(seed: int = 0) -> dict:
    arg_keys = jax.random.split(jax.random.key(seed), 17)
    tokens = bell_draw(arg_keys[0], (TOKENS, D), 1.0, 6.0, ((0, 32),))
    ln1_gain = jnp.clip(1.0 + 0.1 * jax.random.normal(arg_keys[1], (D,), jnp.float32), 0.5, 1.5).astype(jnp.bfloat16)
    ln1_shift = bell_draw(arg_keys[2], (D,), 0.3, 3.0, ((0, 32),))
    qkv_weight = bell_draw(arg_keys[3], (D, 3 * D), D ** -0.5, 0.21875, ((0, 32),))
    qv_bias = bell_draw(arg_keys[4], (2, D), 0.3, 3.0, ((1, 32),))
    proj_weight = bell_draw(arg_keys[5], (D, D), (D * 8 // LEN) ** -0.5, 1.0, ((0, 32),))
    proj_bias = bell_draw(arg_keys[6], (D,), 0.3, 3.0, ((0, 32),))
    ln2_gain = jnp.clip(1.0 + 0.1 * jax.random.normal(arg_keys[7], (D,), jnp.float32), 0.5, 1.5).astype(jnp.bfloat16)
    ln2_shift = bell_draw(arg_keys[8], (D,), 0.3, 3.0, ((0, 32),))
    router_weight = bell_draw(arg_keys[9], (D, EXPERTS), (2 * D) ** -0.5, 0.15625, ((0, 32),))
    expert_in = bell_draw(arg_keys[10], (FF, EXPERTS, D), D ** -0.5, 0.21875, ((0, 32),))
    expert_in_bias = bell_draw(arg_keys[11], (FF, EXPERTS), 0.3, 3.0, ((0, 32),))
    expert_out = bell_draw(arg_keys[12], (FF, EXPERTS, D), (FF // 8) ** -0.5, 0.3125, ((0, 32),))
    expert_out_bias = bell_draw(arg_keys[13], (EXPERTS, D), 0.3, 3.0, ((1, 32),))
    routes_keys = jax.random.split(jax.random.fold_in(arg_keys[14], 1), TOKENS // TOK_DEV)
    routes_turns = jax.random.permutation(jax.random.fold_in(arg_keys[14], 3), TOKENS // TOK_DEV)
    routes = jax.vmap(lambda own, number: deal_out(jax.random.fold_in(arg_keys[14], 2), own, number, TOK_DEV, EXPERTS, TOP, CAP, 1))(routes_keys, routes_turns).reshape((TOKENS, TOP))
    out_grad = heavy_noise(arg_keys[15], (TOKENS, D), 1.0, 6.0, ((0, 32),), (0, 1, 32, 2.75))
    return {"tokens": tokens, "ln1_gain": ln1_gain, "ln1_shift": ln1_shift, "qkv_weight": qkv_weight, "qv_bias": qv_bias, "proj_weight": proj_weight, "proj_bias": proj_bias, "ln2_gain": ln2_gain, "ln2_shift": ln2_shift, "router_weight": router_weight, "expert_in": expert_in, "expert_in_bias": expert_in_bias, "expert_out": expert_out, "expert_out_bias": expert_out_bias, "routes": routes, "out_grad": out_grad}


@jax.custom_vjp
def low(v):
    return lax.optimization_barrier(v.astype(jnp.bfloat16)).astype(jnp.float32)

@jax.custom_vjp
def low_back(v):
    return v

def low_keep(v):
    return (low(v), None)

def low_pass(kept, grad):
    return (grad,)

def back_keep(v):
    return (v, None)

def back_low(kept, grad):
    return (low(grad),)
low.defvjp(low_keep, low_pass)
low_back.defvjp(back_keep, back_low)

def both_ways(values):
    return low(low_back(values))

def layer_norm(values, gain_vec, shift_vec):
    row_mean = lax.optimization_barrier(jnp.mean(values, axis=-1, keepdims=True))
    centred = values - row_mean
    spread = lax.optimization_barrier(jnp.mean(centred * centred, axis=-1, keepdims=True))
    return centred * lax.rsqrt(spread + 1e-06) * gain_vec + shift_vec

def route_index(routes):
    flat_routes = routes.reshape(-1)
    onehot = (flat_routes[:, None] == jnp.arange(EXPERTS, dtype=jnp.int32)[None, :]).astype(jnp.int32)
    before = jnp.cumsum(onehot, axis=0) - onehot
    slot_number = lax.optimization_barrier(jnp.sum(before * onehot, axis=1))
    return (flat_routes * CAP + slot_number).astype(jnp.int32)

def block_forward(inputs, routes, params):
    gain1, shift1, w_qkv, bias_qv, w_proj, bias_proj, gain2, shift2, w_router, w_in, bias_in, w_out, bias_out = params
    highest = lax.Precision.HIGHEST
    row_count = inputs.shape[0]
    shape_four = (SEQ_DEV, LEN, HEADS, HD)
    normed = low(layer_norm(inputs, gain1, shift1))
    projected = jnp.dot(normed, w_qkv, precision=highest)
    queries = both_ways((projected[:, :D] + bias_qv[0]) * HD ** (-0.5))
    key_rows = both_ways(projected[:, D:2 * D])
    values = both_ways(projected[:, 2 * D:] + bias_qv[1])
    scores = low_back(jnp.einsum('sqhd,skhd->shqk', queries.reshape(shape_four), key_rows.reshape(shape_four), precision=highest))
    probs_low = low(jax.nn.softmax(scores, axis=-1))
    attended = jnp.einsum('shqk,skhd->sqhd', probs_low, values.reshape(shape_four), precision=highest)
    attended = both_ways(attended.reshape(row_count, D))
    branch = low_back(jnp.dot(attended, w_proj, precision=highest) + bias_proj)
    middle = inputs + branch
    normed2 = low(layer_norm(middle, gain2, shift2))
    gate_probs = jax.nn.softmax(jnp.dot(normed2, w_router, precision=highest), axis=-1)
    slot_index = route_index(routes)
    onehot = (slot_index[:, None] == jnp.arange(EXPERTS * CAP, dtype=jnp.int32)[None, :]).astype(jnp.float32)
    onehot = onehot.reshape(row_count, TOP, EXPERTS * CAP)
    picks = (routes[:, :, None] == jnp.arange(EXPERTS, dtype=jnp.int32)[None, None, :]).astype(jnp.float32)
    chosen = lax.optimization_barrier(jnp.sum(gate_probs[:, None, :] * picks, axis=2))
    combine = low(lax.optimization_barrier(jnp.sum(onehot * chosen[:, :, None], axis=1)))
    dispatch = lax.optimization_barrier(jnp.sum(onehot, axis=1))
    slot_rows = low_back(jnp.dot(dispatch.T, normed2, precision=highest)).reshape(EXPERTS, CAP, D)
    pre_act = low_back(jnp.einsum('ecd,fed->ecf', slot_rows, w_in, precision=highest) + bias_in.T[:, None, :])
    hidden = low(jax.nn.gelu(pre_act, approximate=True))
    result = both_ways(jnp.einsum('ecf,fed->ecd', hidden, w_out, precision=highest) + bias_out[:, None, :])
    mixture = low_back(jnp.dot(combine, result.reshape(EXPERTS * CAP, D), precision=highest))
    return middle + mixture

def reference(tokens, ln1_gain, ln1_shift, qkv_weight, qv_bias, proj_weight, proj_bias, ln2_gain, ln2_shift, router_weight, expert_in, expert_in_bias, expert_out, expert_out_bias, routes, out_grad):
    weights = tuple((w.astype(jnp.float32) for w in (ln1_gain, ln1_shift, qkv_weight, qv_bias, proj_weight, proj_bias, ln2_gain, ln2_shift, router_weight, expert_in, expert_in_bias, expert_out, expert_out_bias)))
    route_blocks = routes.reshape(N_FSDP, TOK_DEV, TOP)

    def forward(inputs, *params):

        def one_block(carried, block_pair):
            return (carried, jax.checkpoint(block_forward)(block_pair[0], block_pair[1], params))
        _, outputs = lax.scan(one_block, jnp.zeros((), jnp.float32), (inputs.reshape(N_FSDP, TOK_DEV, D), route_blocks))
        return outputs.reshape(TOKENS, D)
    result, pull = jax.vjp(forward, tokens.astype(jnp.float32), *weights)
    grads = pull(out_grad.astype(jnp.float32))
    return (result.astype(jnp.bfloat16), grads[0], grads[1], grads[2], grads[3], grads[4], grads[5], grads[6], grads[7], grads[8], grads[9], grads[10], grads[11], grads[12], grads[13])
```

```python
import functools

import jax
import jax.numpy as jnp
from jax import lax
from jax.sharding import PartitionSpec as P

HEADS = 12
HD = 64
EXPERTS = 4
TOP = 2
LEN = 197
SEQ_DEV = 2
SLOTS = 256
SMALL_ROWS = 8


def layer_norm(values, gain_vec, shift_vec):
    row_mean = jnp.mean(values, axis=-1, keepdims=True)
    centred = values - row_mean
    spread = jnp.mean(centred * centred, axis=-1, keepdims=True)
    return centred * lax.rsqrt(spread + 1e-06) * gain_vec + shift_vec


def gelu_tanh(values):
    return jax.nn.gelu(values, approximate=True)


def take_rows(block, widths):
    pieces, at = [], 0
    for width in widths:
        pieces.append(block[:, at : at + width])
        at += width
    return pieces


def dot_f32(left, right, left_dim, right_dim):
    return lax.dot_general(
        left,
        right,
        (((left_dim,), (right_dim,)), ((), ())),
        preferred_element_type=jnp.float32,
    )


def on_device(
    n_dev,
    tokens,
    ln1_gain,
    ln1_shift,
    qkv_weight,
    qv_bias,
    proj_weight,
    proj_bias,
    ln2_gain,
    ln2_shift,
    router_weight,
    expert_in,
    expert_in_bias,
    expert_out,
    expert_out_bias,
    routes,
    out_grad,
):
    highest = lax.Precision.HIGHEST
    f32 = jnp.float32
    low = jnp.bfloat16
    row_count, model_width = tokens.shape
    shape_four = (SEQ_DEV, LEN, HEADS, HD)
    query_scale = HD ** (-0.5)
    own = qkv_weight.shape[0]
    units = expert_in.shape[0]
    wide = 4 * model_width
    core = lax.axis_index("fsdp") % 2
    same_core = [list(range(c, n_dev, 2)) for c in range(2)]
    swap = [(i, i ^ 1) for i in range(n_dev)]

    small_parts = [
        ln1_gain,
        ln1_shift,
        qv_bias.reshape(-1),
        proj_bias,
        ln2_gain,
        ln2_shift,
        router_weight.T.reshape(-1),
        expert_out_bias.reshape(-1),
        expert_in_bias.T.reshape(-1),
    ]
    small_widths = [p.shape[0] for p in small_parts]
    small_total = sum(small_widths)
    small_mine = jnp.pad(
        jnp.concatenate(small_parts)[None, :], ((0, SMALL_ROWS - 1), (0, wide - small_total))
    )
    dense_mine = jnp.concatenate(
        [jnp.concatenate([qkv_weight, proj_weight], axis=1), small_mine], axis=0
    )
    dense = lax.all_gather(dense_mine, "fsdp", axis=0, tiled=True)
    dense = dense.reshape(n_dev, own + SMALL_ROWS, wide)
    w_in = lax.all_gather(
        expert_in.reshape(units, EXPERTS * model_width),
        "fsdp",
        axis=0,
        tiled=True,
        axis_index_groups=same_core,
    )
    w_out = lax.all_gather(
        expert_out.reshape(units, EXPERTS * model_width),
        "fsdp",
        axis=0,
        tiled=True,
        axis_index_groups=same_core,
    )

    weights = dense[:, :own, :].reshape(n_dev * own, wide)
    w_qkv = weights[:, : 3 * model_width]
    w_proj = weights[:, 3 * model_width :]
    gain1, shift1, bias_qv, bias_proj, gain2, shift2, w_router, bias_out, bias_in = take_rows(
        dense[:, own, :], small_widths
    )
    gain1 = gain1.reshape(-1).astype(f32)
    shift1 = shift1.reshape(-1).astype(f32)
    gain2 = gain2.reshape(-1).astype(f32)
    shift2 = shift2.reshape(-1).astype(f32)
    bias_proj = bias_proj.reshape(-1).astype(f32)
    bias_q = bias_qv[:, :own].reshape(-1).astype(f32)
    bias_v = bias_qv[:, own:].reshape(-1).astype(f32)
    w_router = jnp.stack([p.reshape(-1) for p in take_rows(w_router, [own] * EXPERTS)])
    bias_out = [p.reshape(-1).astype(f32) for p in take_rows(bias_out, [own] * EXPERTS)]
    bias_in = lax.dynamic_index_in_dim(
        bias_in.reshape(n_dev // 2, 2, EXPERTS * units), core, axis=1, keepdims=False
    )
    bias_in = [p.reshape(-1).astype(f32) for p in take_rows(bias_in, [units] * EXPERTS)]

    experts = jnp.arange(EXPERTS, dtype=jnp.int32)[None, :]
    pick = [(routes[:, j : j + 1] == experts).astype(f32) for j in range(TOP)]
    picked = pick[0] + pick[1]
    tri = jnp.arange(row_count)[:, None] > jnp.arange(row_count)[None, :]
    before = dot_f32(tri.astype(low), picked.astype(low), 1, 0)
    slot_ids = jnp.arange(EXPERTS * SLOTS, dtype=jnp.int32)[None, :]
    hit = []
    for j in range(TOP):
        slot = jnp.sum(pick[j] * before, axis=1, keepdims=True).astype(jnp.int32)
        hit.append(slot_ids == routes[:, j : j + 1] * SLOTS + slot)
    dispatch = (hit[0] | hit[1]).astype(low)

    inputs = tokens.astype(f32)
    normed_full, norm1_pull = jax.vjp(layer_norm, inputs, gain1, shift1)
    normed = normed_full.astype(low)
    projected = jnp.dot(normed, w_qkv, preferred_element_type=f32)
    queries = ((projected[:, :model_width] + bias_q) * query_scale).astype(low).reshape(shape_four)
    key_rows = projected[:, model_width : 2 * model_width].astype(low).reshape(shape_four)
    values = (projected[:, 2 * model_width :] + bias_v).astype(low).reshape(shape_four)
    scores = jnp.einsum("sqhd,skhd->shqk", queries, key_rows, preferred_element_type=f32)
    exp_scores = jnp.exp(scores - jnp.max(scores, axis=-1, keepdims=True))
    probs_full = exp_scores / jnp.sum(exp_scores, axis=-1, keepdims=True)
    probs_low = probs_full.astype(low)
    attended = jnp.einsum("shqk,skhd->sqhd", probs_low, values, preferred_element_type=f32)
    attended = attended.reshape(row_count, model_width).astype(low)
    middle = inputs + jnp.dot(attended, w_proj, preferred_element_type=f32) + bias_proj
    normed2_full, norm2_pull = jax.vjp(layer_norm, middle, gain2, shift2)
    normed2 = normed2_full.astype(low)
    gate_probs = jax.nn.softmax(dot_f32(normed2, w_router, 1, 1), axis=-1)
    chosen = [jnp.sum(gate_probs * pick[j], axis=1, keepdims=True) for j in range(TOP)]
    combine = (jnp.where(hit[0], chosen[0], 0.0) + jnp.where(hit[1], chosen[1], 0.0)).astype(low)

    def pair_rows(mine):
        mine = mine.reshape(EXPERTS, SLOTS, model_width)
        theirs = lax.ppermute(mine, "fsdp", swap)
        return [jnp.concatenate([mine[e], theirs[e]], axis=0) for e in range(EXPERTS)]

    def pair_sum(partial):
        sent = jnp.stack([p[SLOTS:].astype(low) for p in partial])
        got = lax.ppermute(sent, "fsdp", swap)
        return [p[:SLOTS] + got[e].astype(f32) for e, p in enumerate(partial)]

    slot_rows = pair_rows(dot_f32(dispatch, normed2, 0, 0).astype(low))
    grad_result_mine = dot_f32(combine, out_grad, 0, 0).astype(low)
    grad_result = pair_rows(grad_result_mine)

    def expert(weight, e):
        return weight[:, e * model_width : (e + 1) * model_width]

    def scatter_units(terms):
        whole = jnp.concatenate([t.astype(low) for t in terms], axis=1)
        return lax.psum_scatter(
            whole, "fsdp", scatter_dimension=0, tiled=True, axis_index_groups=same_core
        )

    each = range(EXPERTS)
    pre_act = [dot_f32(slot_rows[e], expert(w_in, e), 1, 1) + bias_in[e] for e in each]
    hidden, pulls = [], []
    for e in each:
        out, pull = jax.vjp(gelu_tanh, pre_act[e])
        hidden.append(out.astype(low))
        pulls.append(pull)
    expert_out_mine = scatter_units([dot_f32(hidden[e], grad_result[e], 0, 0) for e in each])
    grad_pre = [
        pulls[e](dot_f32(grad_result[e], expert(w_out, e), 1, 1))[0].astype(low) for e in each
    ]
    expert_in_mine = scatter_units([dot_f32(grad_pre[e], slot_rows[e], 0, 0) for e in each])
    grad_bias_in = jnp.stack([jnp.sum(grad_pre[e].astype(f32), axis=0) for e in each])
    summed = pair_sum([dot_f32(hidden[e], expert(w_out, e), 1, 0) for e in each])
    result = jnp.concatenate([(summed[e] + bias_out[e]).astype(low) for e in each], axis=0)
    grad_slots = pair_sum([dot_f32(grad_pre[e], expert(w_in, e), 1, 0) for e in each])
    grad_slots = jnp.concatenate([g.astype(low) for g in grad_slots], axis=0)
    block_out = (middle + jnp.dot(combine, result, preferred_element_type=f32)).astype(low)

    grad_top = out_grad.astype(f32)
    slot_dots = dot_f32(out_grad, result, 1, 1) * dispatch.astype(f32)
    grad_gates = jnp.concatenate(
        [
            jnp.sum(slot_dots[:, e * SLOTS : (e + 1) * SLOTS], axis=1, keepdims=True)
            for e in each
        ],
        axis=1,
    )
    grad_logits = gate_probs * (
        grad_gates - jnp.sum(gate_probs * grad_gates, axis=-1, keepdims=True)
    )
    grad_router = jnp.dot(grad_logits.T, normed2.astype(f32), precision=highest)
    grad_normed2 = jnp.dot(grad_logits, w_router.astype(f32), precision=highest)
    grad_normed2 = grad_normed2 + jnp.dot(dispatch, grad_slots, preferred_element_type=f32)
    grad_mid_norm, grad_gain2, grad_shift2 = norm2_pull(grad_normed2)
    grad_middle = grad_top + grad_mid_norm

    grad_branch = grad_middle.astype(low)
    grad_bias_proj = jnp.sum(grad_branch.astype(f32), axis=0)
    grad_proj = dot_f32(attended, grad_branch, 0, 0)
    grad_attended = dot_f32(grad_branch, w_proj, 1, 1).astype(low).reshape(shape_four)
    grad_probs = jnp.einsum("sqhd,skhd->shqk", grad_attended, values, preferred_element_type=f32)
    grad_values = jnp.einsum(
        "shqk,sqhd->skhd", probs_low, grad_attended, preferred_element_type=f32
    ).astype(low)
    grad_scores = (
        probs_full * (grad_probs - jnp.sum(probs_full * grad_probs, axis=-1, keepdims=True))
    ).astype(low)
    grad_queries = jnp.einsum(
        "shqk,skhd->sqhd", grad_scores, key_rows, preferred_element_type=f32
    ).astype(low)
    grad_keys = jnp.einsum(
        "shqk,sqhd->skhd", grad_scores, queries, preferred_element_type=f32
    ).astype(low)
    grad_query_pre = grad_queries.astype(f32).reshape(row_count, model_width) * query_scale
    grad_values = grad_values.reshape(row_count, model_width)
    grad_projected = jnp.concatenate(
        [grad_query_pre.astype(low), grad_keys.reshape(row_count, model_width), grad_values],
        axis=1,
    )
    grad_qkv = dot_f32(normed, grad_projected, 0, 0)
    grad_normed = dot_f32(grad_projected, w_qkv, 1, 1)
    grad_in_norm, grad_gain1, grad_shift1 = norm1_pull(grad_normed)
    tokens_grad = grad_middle + grad_in_norm

    def by_owner(rows):
        return rows.reshape(-1, n_dev, rows.shape[-1] // n_dev).transpose(1, 0, 2).reshape(n_dev, -1)

    here = (jnp.arange(2) == core).astype(f32)
    bias_in_slots = grad_bias_in.reshape(EXPERTS, n_dev // 2, 1, units) * here[None, None, :, None]
    grad_bias_out = jnp.sum(
        grad_result_mine.astype(f32).reshape(EXPERTS, SLOTS, model_width), axis=1
    )
    small_grads = jnp.concatenate(
        [
            by_owner(
                jnp.concatenate(
                    [
                        jnp.stack(
                            [
                                grad_gain1,
                                grad_shift1,
                                jnp.sum(grad_query_pre, axis=0),
                                jnp.sum(grad_values.astype(f32), axis=0),
                                grad_bias_proj,
                                grad_gain2,
                                grad_shift2,
                            ]
                        ),
                        grad_router,
                        grad_bias_out,
                    ],
                    axis=0,
                )
            ),
            by_owner(bias_in_slots.reshape(EXPERTS, n_dev * units)),
        ],
        axis=1,
    ).astype(low)
    small_grads = jnp.pad(
        small_grads[:, None, :], ((0, 0), (0, SMALL_ROWS - 1), (0, wide - small_total))
    )
    dense_grads = jnp.concatenate([grad_qkv.astype(low), grad_proj.astype(low)], axis=1)
    dense_grads = jnp.concatenate([dense_grads.reshape(n_dev, own, wide), small_grads], axis=1)
    dense_out = lax.psum_scatter(
        dense_grads.reshape(n_dev * (own + SMALL_ROWS), wide),
        "fsdp",
        scatter_dimension=0,
        tiled=True,
    ).astype(f32)
    small = [p[0] for p in take_rows(dense_out[own : own + 1], small_widths)]
    expert_shape = (units, EXPERTS, model_width)
    return (
        block_out,
        tokens_grad,
        small[0],
        small[1],
        dense_out[:own, : 3 * model_width],
        small[2].reshape(2, own),
        dense_out[:own, 3 * model_width :],
        small[3],
        small[4],
        small[5],
        small[6].reshape(EXPERTS, own).T,
        expert_in_mine.astype(f32).reshape(expert_shape),
        small[8].reshape(EXPERTS, units).T,
        expert_out_mine.astype(f32).reshape(expert_shape),
        small[7].reshape(EXPERTS, own),
    )


def solution(mesh):
    in_specs = (
        P("fsdp", None),
        P("fsdp"),
        P("fsdp"),
        P("fsdp", None),
        P(None, "fsdp"),
        P("fsdp", None),
        P("fsdp"),
        P("fsdp"),
        P("fsdp"),
        P("fsdp", None),
        P("fsdp", None, None),
        P("fsdp", None),
        P("fsdp", None, None),
        P(None, "fsdp"),
        P("fsdp", None),
        P("fsdp", None),
    )
    out_specs = (
        P("fsdp", None),
        P("fsdp", None),
        P("fsdp"),
        P("fsdp"),
        P("fsdp", None),
        P(None, "fsdp"),
        P("fsdp", None),
        P("fsdp"),
        P("fsdp"),
        P("fsdp"),
        P("fsdp", None),
        P("fsdp", None, None),
        P("fsdp", None),
        P("fsdp", None, None),
        P(None, "fsdp"),
    )
    return jax.shard_map(
        functools.partial(on_device, mesh.shape["fsdp"]), mesh=mesh, in_specs=in_specs, out_specs=out_specs, check_vma=False
    )
```

```python
import functools

import jax
import jax.numpy as jnp
from jax import lax
from jax.sharding import PartitionSpec as P

HEADS = 12
HD = 64
EXPERTS = 4
TOP = 2
LEN = 197
SEQ_DEV = 2
SLOTS = 256
SMALL_ROWS = 8


def layer_norm(values, gain_vec, shift_vec):
    row_mean = jnp.mean(values, axis=-1, keepdims=True)
    centred = values - row_mean
    spread = jnp.mean(centred * centred, axis=-1, keepdims=True)
    return centred * lax.rsqrt(spread + 1e-06) * gain_vec + shift_vec


def gelu_tanh(values):
    return jax.nn.gelu(values, approximate=True)


def take_rows(block, widths):
    pieces, at = [], 0
    for width in widths:
        pieces.append(block[:, at : at + width])
        at += width
    return pieces


def dot_f32(left, right, left_dim, right_dim):
    return lax.dot_general(
        left,
        right,
        (((left_dim,), (right_dim,)), ((), ())),
        preferred_element_type=jnp.float32,
    )


def on_device(
    n_dev,
    tokens,
    ln1_gain,
    ln1_shift,
    qkv_weight,
    qv_bias,
    proj_weight,
    proj_bias,
    ln2_gain,
    ln2_shift,
    router_weight,
    expert_in,
    expert_in_bias,
    expert_out,
    expert_out_bias,
    routes,
    out_grad,
):
    highest = lax.Precision.HIGHEST
    f32 = jnp.float32
    low = jnp.bfloat16
    row_count, model_width = tokens.shape
    shape_four = (SEQ_DEV, LEN, HEADS, HD)
    query_scale = HD ** (-0.5)
    own = qkv_weight.shape[0]
    units = expert_in.shape[0]
    wide = 4 * model_width
    core = lax.axis_index("fsdp") % 2
    same_core = [list(range(c, n_dev, 2)) for c in range(2)]
    swap = [(i, i ^ 1) for i in range(n_dev)]

    small_parts = [
        ln1_gain,
        ln1_shift,
        qv_bias.reshape(-1),
        proj_bias,
        ln2_gain,
        ln2_shift,
        router_weight.T.reshape(-1),
        expert_out_bias.reshape(-1),
        expert_in_bias.T.reshape(-1),
    ]
    small_widths = [p.shape[0] for p in small_parts]
    small_total = sum(small_widths)
    small_mine = jnp.pad(
        jnp.concatenate(small_parts)[None, :], ((0, SMALL_ROWS - 1), (0, wide - small_total))
    )
    dense_mine = jnp.concatenate(
        [jnp.concatenate([qkv_weight, proj_weight], axis=1), small_mine], axis=0
    )
    dense = lax.all_gather(dense_mine, "fsdp", axis=0, tiled=True)
    dense = dense.reshape(n_dev, own + SMALL_ROWS, wide)
    w_in = lax.all_gather(
        expert_in.reshape(units, EXPERTS * model_width),
        "fsdp",
        axis=0,
        tiled=True,
        axis_index_groups=same_core,
    )
    w_out = lax.all_gather(
        expert_out.reshape(units, EXPERTS * model_width),
        "fsdp",
        axis=0,
        tiled=True,
        axis_index_groups=same_core,
    )

    weights = dense[:, :own, :].reshape(n_dev * own, wide)
    w_qkv = weights[:, : 3 * model_width]
    w_proj = weights[:, 3 * model_width :]
    gain1, shift1, bias_qv, bias_proj, gain2, shift2, w_router, bias_out, bias_in = take_rows(
        dense[:, own, :], small_widths
    )
    gain1 = gain1.reshape(-1).astype(f32)
    shift1 = shift1.reshape(-1).astype(f32)
    gain2 = gain2.reshape(-1).astype(f32)
    shift2 = shift2.reshape(-1).astype(f32)
    bias_proj = bias_proj.reshape(-1).astype(f32)
    bias_q = bias_qv[:, :own].reshape(-1).astype(f32)
    bias_v = bias_qv[:, own:].reshape(-1).astype(f32)
    w_router = jnp.stack([p.reshape(-1) for p in take_rows(w_router, [own] * EXPERTS)])
    bias_out = [p.reshape(-1).astype(f32) for p in take_rows(bias_out, [own] * EXPERTS)]
    bias_in = lax.dynamic_index_in_dim(
        bias_in.reshape(n_dev // 2, 2, EXPERTS * units), core, axis=1, keepdims=False
    )
    bias_in = [p.reshape(-1).astype(f32) for p in take_rows(bias_in, [units] * EXPERTS)]

    experts = jnp.arange(EXPERTS, dtype=jnp.int32)[None, :]
    pick = [(routes[:, j : j + 1] == experts).astype(f32) for j in range(TOP)]
    picked = pick[0] + pick[1]
    tri = jnp.arange(row_count)[:, None] > jnp.arange(row_count)[None, :]
    before = dot_f32(tri.astype(low), picked.astype(low), 1, 0)
    slot_ids = jnp.arange(EXPERTS * SLOTS, dtype=jnp.int32)[None, :]
    hit = []
    for j in range(TOP):
        slot = jnp.sum(pick[j] * before, axis=1, keepdims=True).astype(jnp.int32)
        hit.append(slot_ids == routes[:, j : j + 1] * SLOTS + slot)
    dispatch = (hit[0] | hit[1]).astype(low)

    inputs = tokens.astype(f32)
    normed_full, norm1_pull = jax.vjp(layer_norm, inputs, gain1, shift1)
    normed = normed_full.astype(low)
    projected = jnp.dot(normed, w_qkv, preferred_element_type=f32)
    queries = ((projected[:, :model_width] + bias_q) * query_scale).astype(low).reshape(shape_four)
    key_rows = projected[:, model_width : 2 * model_width].astype(low).reshape(shape_four)
    values = (projected[:, 2 * model_width :] + bias_v).astype(low).reshape(shape_four)
    scores = jnp.einsum("sqhd,skhd->shqk", queries, key_rows, preferred_element_type=f32)
    exp_scores = jnp.exp(scores - jnp.max(scores, axis=-1, keepdims=True))
    probs_full = exp_scores / jnp.sum(exp_scores, axis=-1, keepdims=True)
    probs_low = probs_full.astype(low)
    attended = jnp.einsum("shqk,skhd->sqhd", probs_low, values, preferred_element_type=f32)
    attended = attended.reshape(row_count, model_width).astype(low)
    middle = inputs + jnp.dot(attended, w_proj, preferred_element_type=f32) + bias_proj
    normed2_full, norm2_pull = jax.vjp(layer_norm, middle, gain2, shift2)
    normed2 = normed2_full.astype(low)
    gate_probs = jax.nn.softmax(dot_f32(normed2, w_router, 1, 1), axis=-1)
    chosen = [jnp.sum(gate_probs * pick[j], axis=1, keepdims=True) for j in range(TOP)]
    combine = (jnp.where(hit[0], chosen[0], 0.0) + jnp.where(hit[1], chosen[1], 0.0)).astype(low)

    def pair_rows(mine):
        mine = mine.reshape(EXPERTS, SLOTS, model_width)
        theirs = lax.ppermute(mine, "fsdp", swap)
        return [jnp.concatenate([mine[e], theirs[e]], axis=0) for e in range(EXPERTS)]

    def pair_sum(partial):
        sent = jnp.stack([p[SLOTS:].astype(low) for p in partial])
        got = lax.ppermute(sent, "fsdp", swap)
        return [p[:SLOTS] + got[e].astype(f32) for e, p in enumerate(partial)]

    slot_rows = pair_rows(dot_f32(dispatch, normed2, 0, 0).astype(low))
    grad_result_mine = dot_f32(combine, out_grad, 0, 0).astype(low)
    grad_result = pair_rows(grad_result_mine)

    def expert(weight, e):
        return weight[:, e * model_width : (e + 1) * model_width]

    def scatter_units(terms):
        return lax.psum_scatter(
            terms, "fsdp", scatter_dimension=0, tiled=True, axis_index_groups=same_core
        )

    each = range(EXPERTS)
    pre_act = [dot_f32(slot_rows[e], expert(w_in, e), 1, 1) + bias_in[e] for e in each]
    hidden, pulls = [], []
    for e in each:
        out, pull = jax.vjp(gelu_tanh, pre_act[e])
        hidden.append(out.astype(low))
        pulls.append(pull)
    out_terms = [dot_f32(hidden[e], grad_result[e], 0, 0).astype(low) for e in each]
    out_terms = jnp.concatenate(out_terms, axis=1)
    grad_pre = [
        pulls[e](dot_f32(grad_result[e], expert(w_out, e), 1, 1))[0].astype(low) for e in each
    ]
    in_terms = [dot_f32(grad_pre[e], slot_rows[e], 0, 0).astype(low) for e in each]
    in_terms = jnp.concatenate(in_terms, axis=1)
    out_terms, in_terms, hidden, grad_pre = lax.optimization_barrier(
        (out_terms, in_terms, hidden, grad_pre)
    )
    expert_out_mine = scatter_units(out_terms)
    expert_in_mine = scatter_units(in_terms)
    grad_bias_in = jnp.stack([jnp.sum(grad_pre[e].astype(f32), axis=0) for e in each])
    summed = pair_sum([dot_f32(hidden[e], expert(w_out, e), 1, 0) for e in each])
    result = jnp.concatenate([(summed[e] + bias_out[e]).astype(low) for e in each], axis=0)
    grad_slots = pair_sum([dot_f32(grad_pre[e], expert(w_in, e), 1, 0) for e in each])
    grad_slots = jnp.concatenate([g.astype(low) for g in grad_slots], axis=0)
    block_out = (middle + jnp.dot(combine, result, preferred_element_type=f32)).astype(low)

    grad_top = out_grad.astype(f32)
    slot_dots = dot_f32(out_grad, result, 1, 1) * dispatch.astype(f32)
    grad_gates = jnp.concatenate(
        [
            jnp.sum(slot_dots[:, e * SLOTS : (e + 1) * SLOTS], axis=1, keepdims=True)
            for e in each
        ],
        axis=1,
    )
    grad_logits = gate_probs * (
        grad_gates - jnp.sum(gate_probs * grad_gates, axis=-1, keepdims=True)
    )
    grad_router = jnp.dot(grad_logits.T, normed2.astype(f32), precision=highest)
    grad_normed2 = jnp.dot(grad_logits, w_router.astype(f32), precision=highest)
    grad_normed2 = grad_normed2 + jnp.dot(dispatch, grad_slots, preferred_element_type=f32)
    grad_mid_norm, grad_gain2, grad_shift2 = norm2_pull(grad_normed2)
    grad_middle = grad_top + grad_mid_norm

    grad_branch = grad_middle.astype(low)
    grad_bias_proj = jnp.sum(grad_branch.astype(f32), axis=0)
    grad_proj = dot_f32(attended, grad_branch, 0, 0)
    grad_attended = dot_f32(grad_branch, w_proj, 1, 1).astype(low).reshape(shape_four)
    grad_probs = jnp.einsum("sqhd,skhd->shqk", grad_attended, values, preferred_element_type=f32)
    grad_values = jnp.einsum(
        "shqk,sqhd->skhd", probs_low, grad_attended, preferred_element_type=f32
    ).astype(low)
    grad_scores = (
        probs_full * (grad_probs - jnp.sum(probs_full * grad_probs, axis=-1, keepdims=True))
    ).astype(low)
    grad_queries = jnp.einsum(
        "shqk,skhd->sqhd", grad_scores, key_rows, preferred_element_type=f32
    ).astype(low)
    grad_keys = jnp.einsum(
        "shqk,sqhd->skhd", grad_scores, queries, preferred_element_type=f32
    ).astype(low)
    grad_query_pre = grad_queries.astype(f32).reshape(row_count, model_width) * query_scale
    grad_values = grad_values.reshape(row_count, model_width)
    grad_projected = jnp.concatenate(
        [grad_query_pre.astype(low), grad_keys.reshape(row_count, model_width), grad_values],
        axis=1,
    )
    grad_qkv = dot_f32(normed, grad_projected, 0, 0)
    grad_normed = dot_f32(grad_projected, w_qkv, 1, 1)
    grad_in_norm, grad_gain1, grad_shift1 = norm1_pull(grad_normed)
    tokens_grad = grad_middle + grad_in_norm

    def by_owner(rows):
        return rows.reshape(-1, n_dev, rows.shape[-1] // n_dev).transpose(1, 0, 2).reshape(n_dev, -1)

    here = (jnp.arange(2) == core).astype(f32)
    bias_in_slots = grad_bias_in.reshape(EXPERTS, n_dev // 2, 1, units) * here[None, None, :, None]
    grad_bias_out = jnp.sum(
        grad_result_mine.astype(f32).reshape(EXPERTS, SLOTS, model_width), axis=1
    )
    small_grads = jnp.concatenate(
        [
            by_owner(
                jnp.concatenate(
                    [
                        jnp.stack(
                            [
                                grad_gain1,
                                grad_shift1,
                                jnp.sum(grad_query_pre, axis=0),
                                jnp.sum(grad_values.astype(f32), axis=0),
                                grad_bias_proj,
                                grad_gain2,
                                grad_shift2,
                            ]
                        ),
                        grad_router,
                        grad_bias_out,
                    ],
                    axis=0,
                )
            ),
            by_owner(bias_in_slots.reshape(EXPERTS, n_dev * units)),
        ],
        axis=1,
    ).astype(low)
    small_grads = jnp.pad(
        small_grads[:, None, :], ((0, 0), (0, SMALL_ROWS - 1), (0, wide - small_total))
    )
    dense_grads = jnp.concatenate([grad_qkv.astype(low), grad_proj.astype(low)], axis=1)
    dense_grads = jnp.concatenate([dense_grads.reshape(n_dev, own, wide), small_grads], axis=1)
    dense_grads, expert_out_mine, expert_in_mine = lax.optimization_barrier(
        (dense_grads, expert_out_mine, expert_in_mine)
    )
    dense_out = lax.psum_scatter(
        dense_grads.reshape(n_dev * (own + SMALL_ROWS), wide),
        "fsdp",
        scatter_dimension=0,
        tiled=True,
    ).astype(f32)
    small = [p[0] for p in take_rows(dense_out[own : own + 1], small_widths)]
    expert_shape = (units, EXPERTS, model_width)
    return (
        block_out,
        tokens_grad,
        small[0],
        small[1],
        dense_out[:own, : 3 * model_width],
        small[2].reshape(2, own),
        dense_out[:own, 3 * model_width :],
        small[3],
        small[4],
        small[5],
        small[6].reshape(EXPERTS, own).T,
        expert_in_mine.astype(f32).reshape(expert_shape),
        small[8].reshape(EXPERTS, units).T,
        expert_out_mine.astype(f32).reshape(expert_shape),
        small[7].reshape(EXPERTS, own),
    )


def solution(mesh):
    in_specs = (
        P("fsdp", None),
        P("fsdp"),
        P("fsdp"),
        P("fsdp", None),
        P(None, "fsdp"),
        P("fsdp", None),
        P("fsdp"),
        P("fsdp"),
        P("fsdp"),
        P("fsdp", None),
        P("fsdp", None, None),
        P("fsdp", None),
        P("fsdp", None, None),
        P(None, "fsdp"),
        P("fsdp", None),
        P("fsdp", None),
    )
    out_specs = (
        P("fsdp", None),
        P("fsdp", None),
        P("fsdp"),
        P("fsdp"),
        P("fsdp", None),
        P(None, "fsdp"),
        P("fsdp", None),
        P("fsdp"),
        P("fsdp"),
        P("fsdp"),
        P("fsdp", None),
        P("fsdp", None, None),
        P("fsdp", None),
        P("fsdp", None, None),
        P(None, "fsdp"),
    )
    return jax.shard_map(
        functools.partial(on_device, mesh.shape["fsdp"]), mesh=mesh, in_specs=in_specs, out_specs=out_specs, check_vma=False
    )
```
